128 devices in a mesh: seq: 32 (over y_hi, z, x), wt: 4 (over y_lo, core).
Axes of the slice: x: 4, y: 4 (y_hi: 2, y_lo: 2; y = y_hi * 2 + y_lo), z: 4, core: 2. Of those that a mesh axis runs over, the one named last changes fastest.
Arguments:
- tokens: bfloat16 [4, 8192, 1024], P('wt', 'seq'), may hold values from -6 to 6
- cotangent: bfloat16 [4, 8192, 1024], P('wt', 'seq'), may hold values from -6 to 6
- w_in: float32 [1024, 3, 1024], P('wt', None, 'seq'), may hold values from -0.1875 to 0.1875
- w_out: float32 [1024, 1024], P('wt', 'seq'), may hold values from -0.1875 to 0.1875
- w_mlp: float32 [1024, 2, 4608], P('wt', None, 'seq'), may hold values from -0.1875 to 0.1875
- w_down: float32 [4608, 1024], P('wt', 'seq'), may hold values from -0.09375 to 0.09375
- gains: float32 [2, 1024], replicated, may hold values from 0.5 to 1.5
- taps: float32 [3, 1024], replicated, may hold values from -4 to 4
- m_in: float32 [1024, 3, 1024], P('wt', None, 'seq'), may hold values from -128 to 128
- m_out: float32 [1024, 1024], P('wt', 'seq'), may hold values from -128 to 128
- m_mlp: float32 [1024, 2, 4608], P('wt', None, 'seq'), may hold values from -32 to 32
- m_down: float32 [4608, 1024], P('wt', 'seq'), may hold values from -64 to 64
- m_gains: float32 [2, 1024], replicated, may hold values from -192 to 192
- m_taps: float32 [3, 1024], replicated, may hold values from -128 to 128
- v_in: float32 [1024, 3, 1024], P('wt', None, 'seq'), may hold values from 2490.368 to 9830.4
- v_out: float32 [1024, 1024], P('wt', 'seq'), may hold values from 1723.5968 to 6881.28
- v_mlp: float32 [1024, 2, 4608], P('wt', None, 'seq'), may hold values from 124.5184 to 491.52
- v_down: float32 [4608, 1024], P('wt', 'seq'), may hold values from 622.592 to 2490.368
- v_gains: float32 [2, 1024], replicated, may hold values from 3866.624 to 15400.96
- v_taps: float32 [3, 1024], replicated, may hold values from 2490.368 to 9830.4
Outputs:
- block_out: bfloat16 [4, 8192, 1024], P('wt', 'seq')
- grad_tokens: float32 [4, 8192, 1024], P('wt', 'seq')
- m_in_new: float32 [1024, 3, 1024], P('wt', None, 'seq')
- v_in_new: float32 [1024, 3, 1024], P('wt', None, 'seq')
- w_in_new: float32 [1024, 3, 1024], P('wt', None, 'seq')
- m_out_new: float32 [1024, 1024], P('wt', 'seq')
- v_out_new: float32 [1024, 1024], P('wt', 'seq')
- w_out_new: float32 [1024, 1024], P('wt', 'seq')
- m_mlp_new: float32 [1024, 2, 4608], P('wt', None, 'seq')
- v_mlp_new: float32 [1024, 2, 4608], P('wt', None, 'seq')
- w_mlp_new: float32 [1024, 2, 4608], P('wt', None, 'seq')
- m_down_new: float32 [4608, 1024], P('wt', 'seq')
- v_down_new: float32 [4608, 1024], P('wt', 'seq')
- w_down_new: float32 [4608, 1024], P('wt', 'seq')
- m_gains_new: float32 [2, 1024], replicated
- v_gains_new: float32 [2, 1024], replicated
- gains_new: float32 [2, 1024], replicated
- m_taps_new: float32 [3, 1024], replicated
- v_taps_new: float32 [3, 1024], replicated
- taps_new: float32 [3, 1024], replicated
The draws below stay inside these ranges and needn't reach their ends.
All inputs are finite; a program needn't handle non-finite values.
Results may differ from the reference program's by a relative error of at most 0.033.
Values may be sent and summed in bfloat16 or wider, within the bound.
No kernel may reach another device: no remote copies, remote signals or barrier semaphores. Data moves between devices by JAX's collectives and lax.ppermute only.
A program may use at most 192 MiB of HBM per device.

```python
import math
import jax
import jax.numpy as jnp
from jax import lax

D = 1024
FF = 4608
KERNEL = 3
STEP = 10
LENGTH = 8192
SEQS = 4
TOKENS = 32768


def shard_levels(rng, shape, pieces, smallest, high):
    loudness, own = 1.0, jax.random.fold_in(rng, 6)
    for axis_at, blocks in pieces:
        steps = jnp.exp(jax.random.uniform(jax.random.fold_in(own, axis_at), (blocks,), jnp.float32, smallest / len(pieces), high / len(pieces)))
        loudness = loudness * jnp.repeat(steps, shape[axis_at] // blocks).reshape([-1 if axis == axis_at else 1 for axis in range(len(shape))])
    return loudness


def gaussian(stream_key, extent, deviation, most, shards=(), kind=jnp.bfloat16):
    array = jax.random.normal(stream_key, extent, jnp.float32) * deviation
    if len(shards) > 0:
        array = shard_levels(stream_key, extent, shards, -0.22, 0.18) * array
    return jnp.clip(array, min=-most, max=most).astype(kind)


def setup_inputs(seed: int = 0) -> dict:
    seeds = jax.random.split(jax.random.key(seed), 21)
    tokens = gaussian(seeds[0], (SEQS, LENGTH, D), 1.0, 6.0, ((0, 4), (1, 32)))
    cotangent = gaussian(seeds[1], (SEQS, LENGTH, D), 1.0, 6.0, ((0, 4), (1, 32)))
    w_in = gaussian(seeds[2], (D, 3, D), D ** -0.5, 0.1875, ((0, 4), (2, 32)), jnp.float32)
    w_out = gaussian(seeds[3], (D, D), D ** -0.5, 0.1875, ((0, 4), (1, 32)), jnp.float32)
    w_mlp = gaussian(seeds[4], (D, 2, FF), D ** -0.5, 0.1875, ((0, 4), (2, 32)), jnp.float32)
    w_down = gaussian(seeds[5], (FF, D), FF ** -0.5, 0.09375, ((0, 4), (1, 32)), jnp.float32)
    gains = jnp.clip(1.0 + 0.1 * jax.random.normal(seeds[6], (2, D), jnp.float32), 0.5, 1.5)
    taps = gaussian(seeds[7], (KERNEL, D), 0.6, 4.0, (), jnp.float32)
    m_in = gaussian(seeds[8], (D, 3, D), (0.133 * TOKENS ** 0.5), 128.0, ((0, 4), (2, 32)), jnp.float32)
    m_out = gaussian(seeds[9], (D, D), (0.11 * TOKENS ** 0.5), 128.0, ((0, 4), (1, 32)), jnp.float32)
    m_mlp = gaussian(seeds[10], (D, 2, FF), (0.03 * TOKENS ** 0.5), 32.0, ((0, 4), (2, 32)), jnp.float32)
    m_down = gaussian(seeds[11], (FF, D), (0.067 * TOKENS ** 0.5), 64.0, ((0, 4), (1, 32)), jnp.float32)
    m_gains = gaussian(seeds[12], (2, D), (0.167 * TOKENS ** 0.5), 192.0, (), jnp.float32)
    m_taps = gaussian(seeds[13], (KERNEL, D), (0.133 * TOKENS ** 0.5), 128.0, (), jnp.float32)
    v_in = jnp.clip(jnp.exp(math.log(9830.4) - 1.3730492 * jax.random.uniform(seeds[14], (D, 3, D), jnp.float32) ** shard_levels(seeds[14], (D, 3, D), ((0, 4), (2, 32)), -0.2, 0.2)), 2490.368, 9830.4)
    v_out = jnp.clip(jnp.exp(math.log(6881.28) - 1.3843914 * jax.random.uniform(seeds[15], (D, D), jnp.float32) ** shard_levels(seeds[15], (D, D), ((0, 4), (1, 32)), -0.2, 0.2)), 1723.5968, 6881.28)
    v_mlp = jnp.clip(jnp.exp(math.log(491.52) - 1.3730491 * jax.random.uniform(seeds[16], (D, 2, FF), jnp.float32) ** shard_levels(seeds[16], (D, 2, FF), ((0, 4), (2, 32)), -0.2, 0.2)), 124.5184, 491.52)
    v_down = jnp.clip(jnp.exp(math.log(2490.368) - 1.3862944 * jax.random.uniform(seeds[17], (FF, D), jnp.float32) ** shard_levels(seeds[17], (FF, D), ((0, 4), (1, 32)), -0.2, 0.2)), 622.592, 2490.368)
    v_gains = jnp.clip(jnp.exp(jax.random.uniform(seeds[18], (2, D), jnp.float32, math.log(3866.624), math.log(15400.96))), 3866.624, 15400.96)
    v_taps = jnp.clip(jnp.exp(jax.random.uniform(seeds[19], (KERNEL, D), jnp.float32, math.log(2490.368), math.log(9830.4))), 2490.368, 9830.4)
    return {"tokens": tokens, "cotangent": cotangent, "w_in": w_in, "w_out": w_out, "w_mlp": w_mlp, "w_down": w_down, "gains": gains, "taps": taps, "m_in": m_in, "m_out": m_out, "m_mlp": m_mlp, "m_down": m_down, "m_gains": m_gains, "m_taps": m_taps, "v_in": v_in, "v_out": v_out, "v_mlp": v_mlp, "v_down": v_down, "v_gains": v_gains, "v_taps": v_taps}


EPS = 1e-06
BETA_ONE = 0.9
BETA_TWO = 0.95
ADAM_EPS = 1e-08
DECAY = 0.1

@jax.custom_vjp
def low(v):
    return lax.optimization_barrier(v.astype(jnp.bfloat16)).astype(jnp.float32)

@jax.custom_vjp
def low_back(v):
    return v

def low_keep(v):
    return (low(v), None)

def low_pass(kept, grad):
    return (grad,)

def back_keep(v):
    return (v, None)

def back_low(kept, grad):
    return (low(grad),)
low.defvjp(low_keep, low_pass)
low_back.defvjp(back_keep, back_low)

def matmul(left, right):
    return jnp.dot(left, right, precision=lax.Precision.HIGHEST, preferred_element_type=jnp.float32)

def forward(tok_float, w_in, w_out, w_mlp, w_down, gains, taps):
    seq_len = tok_float.shape[0]
    lag_depth = KERNEL - 1
    hat_one = tok_float * lax.rsqrt(lax.optimization_barrier(jnp.mean(tok_float * tok_float, axis=-1, keepdims=True)) + EPS)
    normed_one = low(hat_one * gains[0])
    projected = low_back(matmul(normed_one, low(w_in).reshape(D, 3 * D)))
    b_part = projected[:, :D]
    c_part = projected[:, D:2 * D]
    x_part = projected[:, 2 * D:]
    product = b_part * x_part
    extended = jnp.concatenate([jnp.zeros((lag_depth, D), jnp.float32), product], axis=0)
    convolved = taps[0] * product
    for lag_step in range(1, KERNEL):
        convolved = convolved + taps[lag_step] * extended[lag_depth - lag_step:lag_depth - lag_step + seq_len]
    mixed = low(c_part * convolved)
    residual_one = tok_float + low_back(matmul(mixed, low(w_out)))
    hat_two = residual_one * lax.rsqrt(lax.optimization_barrier(jnp.mean(residual_one * residual_one, axis=-1, keepdims=True)) + EPS)
    normed_two = low(hat_two * gains[1])
    gate_up = low_back(matmul(normed_two, low(w_mlp).reshape(D, 2 * FF)))
    hidden = low(jax.nn.silu(gate_up[:, :FF]) * gate_up[:, FF:])
    return residual_one + low_back(matmul(hidden, low(w_down)))

def adamw(weight, moment_one, moment_two, grad, rate, decay):
    new_one = BETA_ONE * moment_one + (1.0 - BETA_ONE) * grad
    new_two = BETA_TWO * moment_two + (1.0 - BETA_TWO) * grad * grad
    fixed_one = new_one / (1.0 - BETA_ONE ** STEP)
    fixed_two = new_two / (1.0 - BETA_TWO ** STEP)
    new_weight = weight - rate * (fixed_one / (jnp.sqrt(fixed_two) + ADAM_EPS) + decay * weight)
    return (new_one, new_two, new_weight)

def reference(tokens, cotangent, w_in, w_out, w_mlp, w_down, gains, taps, m_in, m_out, m_mlp, m_down, m_gains, m_taps, v_in, v_out, v_mlp, v_down, v_gains, v_taps):
    weights = (w_in, w_out, w_mlp, w_down, gains, taps)

    def one_sequence(totals, pair):
        seq_tokens, seq_cot = pair
        result, pull = jax.vjp(forward, seq_tokens.astype(jnp.float32), *weights)
        grads = pull(seq_cot.astype(jnp.float32))
        totals = tuple((total + grad for total, grad in zip(totals, grads[1:])))
        return (totals, (result.astype(jnp.bfloat16), grads[0]))
    start = tuple((jnp.zeros(weight.shape, jnp.float32) for weight in weights))
    totals, (block_out, grad_tokens) = lax.scan(one_sequence, start, (tokens, cotangent))
    rates = (0.03, 0.03, 0.03, 0.015, 0.6, 0.5)
    decays = (DECAY, DECAY, DECAY, DECAY, 0.0, 0.0)
    firsts = (m_in, m_out, m_mlp, m_down, m_gains, m_taps)
    seconds = (v_in, v_out, v_mlp, v_down, v_gains, v_taps)
    updated = []
    for index in range(6):
        updated.extend(adamw(weights[index], firsts[index], seconds[index], totals[index], rates[index], decays[index]))
    return (block_out, grad_tokens, updated[0], updated[1], updated[2], updated[3], updated[4], updated[5], updated[6], updated[7], updated[8], updated[9], updated[10], updated[11], updated[12], updated[13], updated[14], updated[15], updated[16], updated[17])
```

```python
import jax
import jax.numpy as jnp
from jax import lax
from jax.sharding import Mesh
from jax.sharding import PartitionSpec as P

D = 1024
FF = 4608
KERNEL = 3
STEP = 10

EPS = 1e-06
BETA_ONE = 0.9
BETA_TWO = 0.95
ADAM_EPS = 1e-08
DECAY = 0.1

SEQ = ("yh", "z", "x")
PLANE = ("z", "x")
ALL = ("yh", "z", "x", "yl", "core")
BF = jnp.bfloat16
F32 = jnp.float32


def flat(yh, z, x, w):
    return ((yh * 4 + z) * 4 + x) * 4 + w


def swapped_place(flip):
    pairs = []
    for s in range(32):
        for w in range(4):
            source = s * 4 + w
            pairs.append((source, flat((s & 1) ^ flip, w, (s >> 1) & 3, s >> 3)))
    return pairs


def straight_place(flip):
    pairs = []
    for s in range(32):
        for w in range(4):
            pairs.append((s * 4 + w, flat((s & 1) ^ flip, s >> 3, (s >> 1) & 3, w)))
    return pairs


def reverse(pairs):
    return [(b, a) for a, b in pairs]


def swap(v, axis):
    return lax.ppermute(v, axis, [(0, 1), (1, 0)])


def gather_group(own):
    far = swap(own, "yl")
    near = swap(own, "core")
    both = swap(far, "core")
    return jnp.stack([own, near, far, both])


def scatter_group(part):
    low = part.astype(BF)
    near = swap(jnp.stack([low[1], low[3]]), "core").astype(F32)
    half = part[2] + near[1]
    far = swap(half.astype(BF), "yl").astype(F32)
    return part[0] + near[0] + far


def place(shard, pairs_of, yh):
    near = lax.ppermute(shard, ALL, pairs_of(0))
    far = lax.ppermute(shard, ALL, pairs_of(1))
    first = jnp.where(yh == 0, near, far)
    second = jnp.where(yh == 0, far, near)
    return jnp.stack([first, second])


def replace(part, pairs_of, yh):
    near = jnp.where(yh == 0, part[0], part[1])
    far = jnp.where(yh == 0, part[1], part[0])
    got_near = lax.ppermute(near, ALL, reverse(pairs_of(0)))
    got_far = lax.ppermute(far, ALL, reverse(pairs_of(1)))
    return got_near.astype(F32) + got_far.astype(F32)


def plane_sum(part):
    shape = part.shape
    own = lax.psum_scatter(
        part.reshape(-1, shape[-1]), PLANE, scatter_dimension=0, tiled=True
    )
    return own.reshape(shape[1:])


def sum_all(v):
    for axis in ("core", "yl", "yh"):
        v = v + swap(v, axis)
    for axis in ("x", "z"):
        got = [
            lax.ppermute(v, axis, [(i, (i + by) % 4) for i in range(4)]) for by in (1, 2, 3)
        ]
        v = v + got[0] + got[1] + got[2]
    return v


def dot_nt(a, b):
    return lax.dot_general(a, b, (((1,), (1,)), ((), ())), preferred_element_type=F32)


def dot_nn(a, b):
    return lax.dot_general(a, b, (((1,), (0,)), ((), ())), preferred_element_type=F32)


def dot_tn(a, b):
    return lax.dot_general(a, b, (((0,), (0,)), ((), ())), preferred_element_type=F32)


def passed_along(shard, by):
    pairs = [(i, i + by) for i in range(32) if 0 <= i + by < 32]
    return lax.ppermute(shard, SEQ, pairs)


def norm_back(grad_hat, hat, scale):
    return scale * (grad_hat - hat * jnp.mean(grad_hat * hat, axis=-1, keepdims=True))


def adamw(weight, moment_one, moment_two, grad, rate, decay):
    new_one = BETA_ONE * moment_one + (1.0 - BETA_ONE) * grad
    new_two = BETA_TWO * moment_two + (1.0 - BETA_TWO) * grad * grad
    fixed_one = new_one / (1.0 - BETA_ONE**STEP)
    fixed_two = new_two / (1.0 - BETA_TWO**STEP)
    new_weight = weight - rate * (fixed_one / (jnp.sqrt(fixed_two) + ADAM_EPS) + decay * weight)
    return (new_one, new_two, new_weight)


def local(
    tokens,
    cotangent,
    w_in,
    w_out,
    w_mlp,
    w_down,
    gains,
    taps,
    m_in,
    m_out,
    m_mlp,
    m_down,
    m_gains,
    m_taps,
    v_in,
    v_out,
    v_mlp,
    v_down,
    v_gains,
    v_taps,
):
    rows = tokens.shape[1]
    lag = KERNEL - 1
    yh = lax.axis_index("yh")
    wt = lax.axis_index(("yl", "core"))
    cw = D // 4
    fw = FF // 4

    t_in = w_in.astype(BF).transpose(1, 2, 0).reshape(96, 256)
    t_mlp = w_mlp.astype(BF).transpose(1, 2, 0).reshape(288, 256)
    t_out = w_out.astype(BF).T
    t_down = w_down.astype(BF).T
    two_in = place(t_in, swapped_place, yh)
    two_out = place(t_out, straight_place, yh)
    two_mlp = place(t_mlp, swapped_place, yh)
    two_down = place(t_down, straight_place, yh)

    toks = gather_group(tokens[0])
    cots = gather_group(cotangent[0])

    two_conv = jnp.concatenate([two_in, two_out], axis=1)
    all_conv = lax.all_gather(two_conv, PLANE, axis=0, tiled=False)
    all_mlp = lax.all_gather(two_mlp, PLANE, axis=0, tiled=False)
    all_down = lax.all_gather(two_down, PLANE, axis=0, tiled=False)

    full_in = (
        all_conv[:, :, :96].reshape(4, 4, 2, 3, 32, 256).transpose(3, 1, 2, 4, 0, 5).reshape(3 * cw, D)
    )
    full_out = all_conv[:, :, 96:].reshape(D, cw)
    full_mlp = (
        all_mlp.reshape(4, 4, 2, 2, 144, 256).transpose(3, 1, 2, 4, 0, 5).reshape(2 * fw, D)
    )
    full_down = all_down.reshape(D, fw)

    tok_all = toks.astype(F32)
    scale_one_all = lax.rsqrt(jnp.mean(tok_all * tok_all, axis=-1, keepdims=True) + EPS)
    hat_one_all = tok_all * scale_one_all
    normed_one = (hat_one_all * gains[0]).astype(BF).reshape(4 * rows, D)

    own_taps = lax.dynamic_slice(taps, (0, wt * cw), (KERNEL, cw))
    projected = dot_nt(normed_one, full_in).reshape(4, rows, 3 * cw)
    b_part = projected[:, :, :cw]
    c_part = projected[:, :, cw : 2 * cw]
    x_part = projected[:, :, 2 * cw :]
    product = b_part * x_part
    before = passed_along(product[:, rows - lag :], 1)
    extended = jnp.concatenate([before, product], axis=1)
    convolved = own_taps[0] * product
    for k in range(1, KERNEL):
        convolved = convolved + own_taps[k] * extended[:, lag - k : lag - k + rows]
    mixed = (c_part * convolved).astype(BF).reshape(4 * rows, cw)
    branch = dot_nt(mixed, full_out).reshape(4, rows, D)
    residual = tokens[0].astype(F32) + scatter_group(branch)
    scale_two = lax.rsqrt(jnp.mean(residual * residual, axis=-1, keepdims=True) + EPS)
    hat_two = residual * scale_two
    normed_two = gather_group((hat_two * gains[1]).astype(BF)).reshape(4 * rows, D)
    gate_up = dot_nt(normed_two, full_mlp)
    gate = gate_up[:, :fw]
    up = gate_up[:, fw:]
    sig = jax.nn.sigmoid(gate)
    swished = gate * sig
    hidden = (swished * up).astype(BF)
    down = dot_nt(hidden, full_down).reshape(4, rows, D)
    block_out = (residual + scatter_group(down)).astype(BF)[None]

    cot_flat = cots.reshape(4 * rows, D)
    grad_down = dot_tn(cot_flat, hidden).astype(BF)
    grad_hidden = dot_nn(cot_flat, full_down)
    grad_up = grad_hidden * swished
    grad_gate = grad_hidden * up * sig * (1.0 + gate * (1.0 - sig))
    grad_gu = jnp.concatenate([grad_gate, grad_up], axis=1).astype(BF)
    grad_normed_two = scatter_group(dot_nn(grad_gu, full_mlp).reshape(4, rows, D))
    sum_down = plane_sum(grad_down.reshape(16, 2, 32, fw))
    grad_mlp = dot_tn(grad_gu, normed_two).astype(BF)
    grad_mlp = (
        grad_mlp.reshape(2, 4, 2, 144, 4, 256).transpose(4, 1, 2, 0, 3, 5).reshape(16, 2, 288, 256)
    )
    sum_mlp = plane_sum(grad_mlp)
    gain_two = jnp.sum(grad_normed_two * hat_two, axis=0)
    grad_resid = cotangent[0].astype(F32) + norm_back(
        grad_normed_two * gains[1], hat_two, scale_two
    )
    branch_all = gather_group(grad_resid.astype(BF)).reshape(4 * rows, D)
    grad_mixed = dot_nn(branch_all, full_out).reshape(4, rows, cw)
    grad_out = dot_tn(branch_all, mixed).astype(BF)
    grad_c = grad_mixed * convolved
    grad_conv = grad_mixed * c_part
    after = passed_along(grad_conv[:, :lag], -1)
    ext_grad = jnp.concatenate([grad_conv, after], axis=1)
    grad_product = own_taps[0] * grad_conv
    tap_rows = [jnp.sum(grad_conv * product, axis=(0, 1))]
    for k in range(1, KERNEL):
        grad_product = grad_product + own_taps[k] * ext_grad[:, k : k + rows]
        tap_rows.append(jnp.sum(grad_conv * extended[:, lag - k : lag - k + rows], axis=(0, 1)))
    grad_b = grad_product * x_part
    grad_x = grad_product * b_part
    grad_proj = (
        jnp.concatenate([grad_b, grad_c, grad_x], axis=2).astype(BF).reshape(4 * rows, 3 * cw)
    )
    grad_in = dot_tn(grad_proj, normed_one).astype(BF)
    grad_in = (
        grad_in.reshape(3, 4, 2, 32, 4, 256).transpose(4, 1, 2, 0, 3, 5).reshape(16, 2, 96, 256)
    )
    grad_out = grad_out.reshape(16, 2, 32, 256)
    sum_conv = plane_sum(jnp.concatenate([grad_in, grad_out], axis=2))
    part_one = dot_nn(grad_proj, full_in).reshape(4, rows, D)
    gain_one = jnp.sum(part_one * hat_one_all, axis=(0, 1))
    grad_normed_one = scatter_group(part_one)
    hat_one = hat_one_all[0]
    grad_input = grad_resid + norm_back(
        grad_normed_one * gains[0], hat_one, scale_one_all[0]
    )

    tap_full = lax.dynamic_update_slice(
        jnp.zeros((KERNEL, D), F32), jnp.stack(tap_rows), (0, wt * cw)
    )
    small = sum_all(jnp.concatenate([gain_one[None], gain_two[None], tap_full], axis=0))

    total_down = replace(sum_down, straight_place, yh).T
    total_mlp = replace(sum_mlp, swapped_place, yh).reshape(2, 144, 256).transpose(2, 0, 1)
    total_in = replace(sum_conv[:, :96], swapped_place, yh).reshape(3, 32, 256).transpose(2, 0, 1)
    total_out = replace(sum_conv[:, 96:], straight_place, yh).T
    new_in = adamw(w_in, m_in, v_in, total_in, 0.03, DECAY)
    new_out = adamw(w_out, m_out, v_out, total_out, 0.03, DECAY)
    new_mlp = adamw(w_mlp, m_mlp, v_mlp, total_mlp, 0.03, DECAY)
    new_down = adamw(w_down, m_down, v_down, total_down, 0.015, DECAY)
    new_gains = adamw(gains, m_gains, v_gains, small[:2], 0.6, 0.0)
    new_taps = adamw(taps, m_taps, v_taps, small[2:], 0.5, 0.0)
    return (
        block_out,
        grad_input[None],
        *new_in,
        *new_out,
        *new_mlp,
        *new_down,
        *new_gains,
        *new_taps,
    )


def solution(mesh):
    fine = Mesh(mesh.devices.reshape(2, 4, 4, 2, 2), ALL)
    wt = ("yl", "core")
    acts = P(wt, SEQ, None)
    cube = P(wt, None, SEQ)
    flat_w = P(wt, SEQ)
    weights = (cube, flat_w, cube, flat_w, P(), P())
    in_specs = (acts, acts) + weights * 3
    out_specs = (acts, acts)
    for spec in weights:
        out_specs = out_specs + (spec, spec, spec)
    return jax.shard_map(local, mesh=fine, in_specs=in_specs, out_specs=out_specs, check_vma=False)
```

```python
import jax
import jax.numpy as jnp
from jax import lax
from jax.experimental import pallas as pl
from jax.experimental.pallas import tpu as pltpu
from jax.sharding import Mesh
from jax.sharding import PartitionSpec as P

D = 1024
FF = 4608
KERNEL = 3
STEP = 10

EPS = 1e-06
BETA_ONE = 0.9
BETA_TWO = 0.95
ADAM_EPS = 1e-08
DECAY = 0.1

SEQ = ("yh", "z", "x")
PLANE = ("z", "x")
ALL = ("yh", "z", "x", "yl", "core")
BF = jnp.bfloat16
F32 = jnp.float32


def flat(yh, z, x, w):
    return ((yh * 4 + z) * 4 + x) * 4 + w


def swapped_place(flip):
    pairs = []
    for s in range(32):
        for w in range(4):
            source = s * 4 + w
            pairs.append((source, flat((s & 1) ^ flip, w, (s >> 1) & 3, s >> 3)))
    return pairs


def straight_place(flip):
    pairs = []
    for s in range(32):
        for w in range(4):
            pairs.append((s * 4 + w, flat((s & 1) ^ flip, s >> 3, (s >> 1) & 3, w)))
    return pairs


def reverse(pairs):
    return [(b, a) for a, b in pairs]


def swap(v, axis):
    return lax.ppermute(v, axis, [(0, 1), (1, 0)])


def gather_group(own):
    far = swap(own, "yl")
    near = swap(own, "core")
    both = swap(far, "core")
    return jnp.stack([own, near, far, both])


def scatter_group(keep, low):
    near = swap(low, "core").astype(F32)
    half = keep[1] + near[1]
    far = swap(half.astype(BF), "yl").astype(F32)
    return keep[0] + near[0] + far


def tie(*values):
    return lax.optimization_barrier(values)


def in_order(near, far, yh):
    first = jnp.where(yh == 0, near, far)
    second = jnp.where(yh == 0, far, near)
    return jnp.stack([first, second])


def replace(first, second, pairs_of, yh):
    near = jnp.where(yh == 0, first, second)
    far = jnp.where(yh == 0, second, first)
    got_near = lax.ppermute(near, ALL, reverse(pairs_of(0)))
    got_far = lax.ppermute(far, ALL, reverse(pairs_of(1)))
    return got_near.astype(F32) + got_far.astype(F32)


def tn_kernel(a_ref, b_ref, out_ref):
    full = lax.dot_general(
        a_ref[...], b_ref[...], (((0,), (0,)), ((), ())), preferred_element_type=F32
    )
    for k in range(4):
        out_ref[k] = full[:, 256 * k : 256 * (k + 1)].astype(BF)


def dot_tn_blocked(a, b, step):
    rows, wide = a.shape
    return pl.pallas_call(
        tn_kernel,
        grid=(wide // step,),
        in_specs=[
            pl.BlockSpec((rows, step), lambda i: (0, i)),
            pl.BlockSpec((rows, D), lambda i: (0, 0)),
        ],
        out_specs=pl.BlockSpec((4, step, 256), lambda i: (0, i, 0)),
        out_shape=jax.ShapeDtypeStruct((4, wide, 256), BF),
        compiler_params=pltpu.CompilerParams(vmem_limit_bytes=40 * 1024 * 1024),
        cost_estimate=pl.CostEstimate(
            flops=2 * rows * wide * D,
            bytes_accessed=2 * (rows * wide + rows * D + wide * D),
            transcendentals=0,
        ),
    )(a, b)


def dot_nt(a, b):
    return lax.dot_general(a, b, (((1,), (1,)), ((), ())), preferred_element_type=F32)


def dot_nn(a, b):
    return lax.dot_general(a, b, (((1,), (0,)), ((), ())), preferred_element_type=F32)


def dot_tn(a, b):
    return lax.dot_general(a, b, (((0,), (0,)), ((), ())), preferred_element_type=F32)


def unit_rows(v):
    return v * lax.rsqrt(jnp.mean(v * v, axis=-1, keepdims=True) + EPS)


def in_part(w_ref, k, part):
    return w_ref[k, :, :, 32 * part : 32 * part + 32].reshape(256, 256)


def conv_kernel(
    tok_ref, halo_ref, gain_ref, tap_ref, w_ref, n_ref, p_ref, bx_ref, z_ref, y_ref, keep_ref, low_ref
):
    rows = n_ref.shape[1]
    tok = jnp.concatenate([halo_ref[0], tok_ref[0]], axis=0).astype(F32)
    normed = (unit_rows(tok) * gain_ref[0:1, :]).astype(BF)
    n_ref[0] = normed[16:]
    parts = []
    for part in range(3):
        weight = jnp.concatenate([in_part(w_ref, k, part) for k in range(4)], axis=1)
        parts.append(dot_nt(normed, weight))
        p_ref[0, part] = parts[part][16:]
    product = parts[0] * parts[2]
    bx_ref[0] = product
    conv = tap_ref[0:1, :] * product[16:]
    for k in range(1, KERNEL):
        conv = conv + tap_ref[k : k + 1, :] * product[16 - k : 16 - k + rows]
    z_ref[0] = conv
    mixed = (parts[1][16:] * conv).astype(BF)
    y_ref[0] = mixed
    put_part(dot_nt(mixed, w_ref[:, :, :, 96:128].reshape(D, 256)), keep_ref, low_ref)


def spec_of(shape, mode):
    tail = (0,) * (len(shape) - 1)
    if mode == "whole":
        return pl.BlockSpec(shape, lambda i: (0,) + tail)
    if mode == "two":
        return pl.BlockSpec((2,) + tuple(shape[1:]), lambda i: (i,) + tail)
    if mode == "pair":
        return pl.BlockSpec((1,) + tuple(shape[1:]), lambda i: (i // 2,) + tail)
    return pl.BlockSpec((1,) + tuple(shape[1:]), lambda i: (i,) + tail)


def grid_call(kernel, steps, ins, outs, flops, scratch=()):
    moved = sum(v.size * v.dtype.itemsize for v, _ in ins + outs)
    return pl.pallas_call(
        kernel,
        grid=(steps,),
        in_specs=[spec_of(v.shape, mode) for v, mode in ins],
        out_specs=[spec_of(v.shape, mode) for v, mode in outs],
        out_shape=[v for v, _ in outs],
        scratch_shapes=list(scratch),
        compiler_params=pltpu.CompilerParams(vmem_limit_bytes=56 * 1024 * 1024),
        cost_estimate=pl.CostEstimate(flops=flops, bytes_accessed=moved, transcendentals=0),
    )(*[v for v, _ in ins])


def put_part(value, keep_ref, low_ref):
    step = pl.program_id(0)

    @pl.when(step % 2 == 0)
    def _():
        keep_ref[0] = value

    @pl.when(step % 2 == 1)
    def _():
        low_ref[0] = value.astype(BF)


def ff_grad_kernel(g_ref, n_ref, c_ref, q_ref, out_ref):
    step = pl.program_id(0)
    for part in range(2):

        @pl.when(step == part)
        def _():
            full = lax.dot_general(
                g_ref[...], n_ref[...], (((0,), (0,)), ((), ())), preferred_element_type=F32
            ).astype(BF)
            for k in range(8):
                start = 288 * (k % 2) + 144 * part
                out_ref[k // 2, :, start : start + 144] = full[
                    :, 128 * k : 128 * (k + 1)
                ].reshape(8, 144, 128)

    @pl.when(step == 2)
    def _():
        full = lax.dot_general(
            c_ref[...], q_ref[...], (((0,), (0,)), ((), ())), preferred_element_type=F32
        ).astype(BF)
        for k in range(9):
            out_ref[:, :, 576 + 32 * k : 608 + 32 * k] = full[
                :, 128 * k : 128 * (k + 1)
            ].reshape(4, 8, 32, 128)


def ff_grads(g, n, c, q):
    rows, fw = q.shape
    return pl.pallas_call(
        ff_grad_kernel,
        grid=(3,),
        in_specs=[
            pl.BlockSpec((rows, fw), lambda i: (0, jnp.minimum(i, 1))),
            spec_of(n.shape, "whole"),
            spec_of(c.shape, "whole"),
            spec_of(q.shape, "whole"),
        ],
        out_specs=spec_of((4, 8, 864, 128), "whole"),
        out_shape=jax.ShapeDtypeStruct((4, 8, 864, 128), BF),
        compiler_params=pltpu.CompilerParams(vmem_limit_bytes=56 * 1024 * 1024),
        cost_estimate=pl.CostEstimate(
            flops=6 * rows * fw * D, bytes_accessed=19 * 1024 * 1024, transcendentals=0
        ),
    )(g, n, c, q)


def mlp_kernel(
    n_ref, c_ref, w_ref, q_ref, g_ref, down_ref, down_low, back_ref, back_low, up_w, down_w
):
    fw = FF // 4
    rows = n_ref.shape[1]

    @pl.when(pl.program_id(0) == 0)
    def _():
        for k in range(8):
            for part in range(2):
                start = 288 * (k % 2) + 144 * part
                up_w[fw * part : fw * (part + 1), 128 * k : 128 * (k + 1)] = w_ref[
                    k // 2, :, :, start : start + 144
                ].reshape(fw, 128)
        for k in range(9):
            down_w[:, 128 * k : 128 * (k + 1)] = w_ref[
                :, :, :, 576 + 32 * k : 608 + 32 * k
            ].reshape(D, 128)

    normed = n_ref[...].reshape(2 * rows, D)
    cot = c_ref[...].reshape(2 * rows, D)
    down = None
    back = None
    wide = 384
    for j in range(fw // wide):
        cols = slice(wide * j, wide * (j + 1))
        gate_w = up_w[wide * j : wide * (j + 1), :]
        lift_w = up_w[fw + wide * j : fw + wide * (j + 1), :]
        drop_w = down_w[:, cols]
        gate = dot_nt(normed, gate_w)
        lift = dot_nt(normed, lift_w)
        grad_hidden = dot_nn(cot, drop_w)
        sig = jax.nn.sigmoid(gate)
        swished = gate * sig
        hidden = (swished * lift).astype(BF)
        grad_lift = (grad_hidden * swished).astype(BF)
        grad_gate = (grad_hidden * lift * sig * (1.0 + gate * (1.0 - sig))).astype(BF)
        q_ref[:, :, cols] = hidden.reshape(2, rows, wide)
        g_ref[:, :, cols] = grad_gate.reshape(2, rows, wide)
        g_ref[:, :, fw + wide * j : fw + wide * (j + 1)] = grad_lift.reshape(2, rows, wide)
        more_down = dot_nt(hidden, drop_w)
        more_back = dot_nn(grad_gate, gate_w) + dot_nn(grad_lift, lift_w)
        down = more_down if j == 0 else down + more_down
        back = more_back if j == 0 else back + more_back
    down_ref[0] = down[:rows]
    down_low[0] = down[rows:].astype(BF)
    back_ref[0] = back[:rows]
    back_low[0] = back[rows:].astype(BF)


def mix_back_kernel(do_ref, w_ref, p_ref, z_ref, dz_ref, dc_ref):
    grad = dot_nn(do_ref[0], w_ref[:, :, :, 96:128].reshape(D, 256))
    dc_ref[0] = (grad * z_ref[0]).astype(BF)
    dz_ref[0] = grad * p_ref[0, 1]


def conv_back_kernel(
    dz_ref, after_ref, bx_ref, p_ref, dc_ref, tap_ref, tok_ref, w_ref, dp_ref, keep_ref, low_ref, gain_ref, gtap_ref
):
    rows = dz_ref.shape[1]
    dz = dz_ref[0]
    extended = jnp.concatenate([dz, after_ref[0]], axis=0)
    product = bx_ref[0]
    grad = tap_ref[0:1, :] * dz
    sums = [jnp.sum(dz * product[16:], axis=0, keepdims=True)]
    for k in range(1, KERNEL):
        grad = grad + tap_ref[k : k + 1, :] * extended[k : k + rows]
        sums.append(jnp.sum(dz * product[16 - k : 16 - k + rows], axis=0, keepdims=True))
    parts = [(grad * p_ref[0, 2]).astype(BF), dc_ref[0], (grad * p_ref[0, 0]).astype(BF)]
    for part in range(3):
        dp_ref[0, :, 256 * part : 256 * (part + 1)] = parts[part]
    all_parts = jnp.concatenate(parts, axis=1)
    hat = unit_rows(tok_ref[0].astype(F32))
    gains = []
    pieces = []
    for k in range(4):
        weight = jnp.concatenate([in_part(w_ref, k, part) for part in range(3)], axis=0)
        back = dot_nn(all_parts, weight)
        pieces.append(back)
        gains.append(
            jnp.sum(back * hat[:, 256 * k : 256 * (k + 1)], axis=0, keepdims=True)
        )
    put_part(jnp.concatenate(pieces, axis=1), keep_ref, low_ref)
    gain = jnp.concatenate(gains, axis=1)
    tap = jnp.concatenate(sums, axis=0)

    @pl.when(pl.program_id(0) == 0)
    def _():
        gain_ref[...] = gain
        gtap_ref[...] = tap

    @pl.when(pl.program_id(0) > 0)
    def _():
        gain_ref[...] += gain
        gtap_ref[...] += tap


def passed_along(shard, by):
    pairs = [(i, i + by) for i in range(32) if 0 <= i + by < 32]
    return lax.ppermute(shard, SEQ, pairs)


def norm_back(grad_hat, hat, scale):
    return scale * (grad_hat - hat * jnp.mean(grad_hat * hat, axis=-1, keepdims=True))


def adamw(weight, moment_one, moment_two, grad, rate, decay):
    new_one = BETA_ONE * moment_one + (1.0 - BETA_ONE) * grad
    new_two = BETA_TWO * moment_two + (1.0 - BETA_TWO) * grad * grad
    fixed_one = new_one / (1.0 - BETA_ONE**STEP)
    fixed_two = new_two / (1.0 - BETA_TWO**STEP)
    new_weight = weight - rate * (fixed_one / (jnp.sqrt(fixed_two) + ADAM_EPS) + decay * weight)
    return (new_one, new_two, new_weight)


def local(
    tokens,
    cotangent,
    w_in,
    w_out,
    w_mlp,
    w_down,
    gains,
    taps,
    m_in,
    m_out,
    m_mlp,
    m_down,
    m_gains,
    m_taps,
    v_in,
    v_out,
    v_mlp,
    v_down,
    v_gains,
    v_taps,
):
    rows = tokens.shape[1]
    yh = lax.axis_index("yh")
    wt = lax.axis_index(("yl", "core"))
    cw = D // 4
    fw = FF // 4

    t_in = w_in.astype(BF).transpose(1, 2, 0).reshape(96, 256)
    t_mlp = w_mlp.astype(BF).transpose(1, 2, 0).reshape(288, 256)
    t_out = w_out.astype(BF).T
    t_down = w_down.astype(BF).T
    t_swapped = jnp.concatenate([t_in, t_mlp], axis=0)
    t_straight = jnp.concatenate([t_out, t_down], axis=1)
    own_toks = tokens[0]
    moved = [
        lax.ppermute(t_swapped, ALL, swapped_place(0)),
        lax.ppermute(t_swapped, ALL, swapped_place(1)),
        lax.ppermute(t_straight, ALL, straight_place(0)),
        lax.ppermute(t_straight, ALL, straight_place(1)),
        swap(own_toks, "yl"),
        swap(own_toks, "core"),
        passed_along(own_toks[rows - 16 :], 1),
    ]
    moved = tie(*moved)
    two_swapped = in_order(moved[0], moved[1], yh)
    two_straight = in_order(moved[2], moved[3], yh)
    two_conv = jnp.concatenate([two_swapped[:, :96], two_straight[:, :, :256]], axis=1)
    mlp_rows = two_swapped[:, 96:]
    two_ff = jnp.concatenate(
        [mlp_rows[:, :, :128], mlp_rows[:, :, 128:]]
        + [two_straight[:, :, 256 + 128 * k : 384 + 128 * k] for k in range(9)],
        axis=1,
    )
    toks = jnp.stack([own_toks, moved[5], moved[4], swap(moved[4], "core")])
    halo = gather_group(moved[6])
    cots = gather_group(cotangent[0])

    sent = jnp.broadcast_to(two_conv.reshape(1, 256, 256), (16, 256, 256)).reshape(4096, 256)
    all_conv = lax.all_to_all(sent, PLANE, split_axis=0, concat_axis=0, tiled=True)
    all_conv = all_conv.reshape(4, 4, 2, 128, 256)
    all_ff = lax.all_gather(two_ff, PLANE, axis=0, tiled=False).reshape(4, 4, 2, 864, 128)

    own_taps = lax.dynamic_slice(taps, (0, wt * cw), (KERNEL, cw))
    shape = jax.ShapeDtypeStruct
    normed_one, parts, product, convolved, mixed, branch, branch_low = grid_call(
        conv_kernel,
        4,
        [
            (toks, "row"),
            (halo, "row"),
            (gains, "whole"),
            (own_taps, "whole"),
            (all_conv, "whole"),
        ],
        [
            (shape((4, rows, D), BF), "row"),
            (shape((4, 3, rows, cw), F32), "row"),
            (shape((4, rows + 16, cw), F32), "row"),
            (shape((4, rows, cw), F32), "row"),
            (shape((4, rows, cw), BF), "row"),
            (shape((2, rows, D), F32), "pair"),
            (shape((2, rows, D), BF), "pair"),
        ],
        8 * rows * D * D,
    )
    branch_low, cots = tie(branch_low, cots)
    residual = tokens[0].astype(F32) + scatter_group(branch, branch_low)
    scale_two = lax.rsqrt(jnp.mean(residual * residual, axis=-1, keepdims=True) + EPS)
    hat_two = residual * scale_two
    normed_two = gather_group((hat_two * gains[1]).astype(BF))
    hidden, grad_gu, down, down_low, back, back_low = grid_call(
        mlp_kernel,
        2,
        [(normed_two, "two"), (cots, "two"), (all_ff, "whole")],
        [
            (shape((4, rows, fw), BF), "two"),
            (shape((4, rows, 2 * fw), BF), "two"),
            (shape((2, rows, D), F32), "row"),
            (shape((2, rows, D), BF), "row"),
            (shape((2, rows, D), F32), "row"),
            (shape((2, rows, D), BF), "row"),
        ],
        48 * rows * D * fw,
        [pltpu.VMEM((2 * fw, D), BF), pltpu.VMEM((D, fw), BF)],
    )
    near = swap(back_low, "core").astype(F32)
    back_half = (back[1] + near[1]).astype(BF)
    back_half, grad_gu = tie(back_half, grad_gu)
    back_far = swap(back_half, "yl")
    ff = ff_grads(
        grad_gu.reshape(4 * rows, 2 * fw),
        normed_two.reshape(4 * rows, D),
        cots.reshape(4 * rows, D),
        hidden.reshape(4 * rows, fw),
    )
    sum_ff = lax.psum_scatter(
        ff.reshape(16 * 1728, 128), PLANE, scatter_dimension=0, tiled=True
    ).reshape(2, 864, 128)
    grad_normed_two = back[0] + near[0] + back_far.astype(F32)
    gain_two = jnp.sum(grad_normed_two * hat_two, axis=0)
    grad_resid = cotangent[0].astype(F32) + norm_back(
        grad_normed_two * gains[1], hat_two, scale_two
    )
    branch_all = gather_group(grad_resid.astype(BF))
    grad_conv, grad_c = grid_call(
        mix_back_kernel,
        4,
        [(branch_all, "row"), (all_conv, "whole"), (parts, "row"), (convolved, "row")],
        [(shape((4, rows, cw), F32), "row"), (shape((4, rows, cw), BF), "row")],
        2 * rows * D * D,
    )
    grad_conv, down_low = tie(grad_conv, down_low)
    after = passed_along(grad_conv[:, :8], -1)
    block_out = (residual + scatter_group(down, down_low)).astype(BF)[None]
    grad_proj, part_one, part_low, gain_one, tap_sums = grid_call(
        conv_back_kernel,
        4,
        [
            (grad_conv, "row"),
            (after, "row"),
            (product, "row"),
            (parts, "row"),
            (grad_c, "row"),
            (own_taps, "whole"),
            (toks, "row"),
            (all_conv, "whole"),
        ],
        [
            (shape((4, rows, 3 * cw), BF), "row"),
            (shape((2, rows, D), F32), "pair"),
            (shape((2, rows, D), BF), "pair"),
            (shape((1, D), F32), "whole"),
            (shape((KERNEL, cw), F32), "whole"),
        ],
        6 * rows * D * D,
    )
    grad_out = dot_tn(branch_all.reshape(4 * rows, D), mixed.reshape(4 * rows, cw)).astype(BF)
    grad_in = dot_tn_blocked(
        grad_proj.reshape(4 * rows, 3 * cw), normed_one.reshape(4 * rows, D), 384
    ).reshape(4, 3, 4, 2, 32, 256)
    grad_in = grad_in.transpose(3, 0, 2, 1, 4, 5).reshape(32, 96, 256)
    grad_conv_w = jnp.concatenate([grad_in, grad_out.reshape(32, 32, 256)], axis=1)
    tap_full = lax.dynamic_update_slice(jnp.zeros((KERNEL, D), F32), tap_sums, (0, wt * cw))
    small = jnp.concatenate([gain_one, gain_two[None], tap_full], axis=0).reshape(20, 256)
    small = jnp.pad(small.astype(BF), ((0, 12), (0, 0)))
    grad_conv_w = jnp.concatenate(
        [grad_conv_w, jnp.broadcast_to(small[None], (32, 32, 256))], axis=1
    )
    got_conv = lax.all_to_all(
        grad_conv_w.reshape(32 * 160, 256), SEQ, split_axis=0, concat_axis=0, tiled=True
    )
    total_mlp = replace(sum_ff[0, :576], sum_ff[1, :576], swapped_place, yh)
    total_down = replace(sum_ff[0, 576:], sum_ff[1, 576:], straight_place, yh)
    got_conv, total_mlp, total_down = tie(got_conv, total_mlp, total_down)
    sum_conv = jnp.sum(got_conv.reshape(32, 160, 256).astype(F32), axis=0)
    small = sum_conv[128:148]
    small = small + swap(small, "core")
    small = (small + swap(small, "yl")).reshape(5, D)
    grad_normed_one = scatter_group(part_one, part_low)
    tok_float = tokens[0].astype(F32)
    scale_one = lax.rsqrt(jnp.mean(tok_float * tok_float, axis=-1, keepdims=True) + EPS)
    hat_one = tok_float * scale_one
    grad_input = grad_resid + norm_back(grad_normed_one * gains[0], hat_one, scale_one)
    total_mlp = total_mlp.reshape(2, 2, 144, 128).transpose(0, 3, 1, 2).reshape(256, 2, 144)
    total_down = total_down.reshape(9, 32, 128).transpose(0, 2, 1).reshape(fw, 32)
    total_in = lax.ppermute(sum_conv[:96], ALL, reverse(swapped_place(0)))
    total_in = total_in.reshape(3, 32, 256).transpose(2, 0, 1)
    total_out = sum_conv[96:128].T
    new_in = adamw(w_in, m_in, v_in, total_in, 0.03, DECAY)
    new_out = adamw(w_out, m_out, v_out, total_out, 0.03, DECAY)
    new_mlp = adamw(w_mlp, m_mlp, v_mlp, total_mlp, 0.03, DECAY)
    new_down = adamw(w_down, m_down, v_down, total_down, 0.015, DECAY)
    new_gains = adamw(gains, m_gains, v_gains, small[:2], 0.6, 0.0)
    new_taps = adamw(taps, m_taps, v_taps, small[2:], 0.5, 0.0)
    return (
        block_out,
        grad_input[None],
        *new_in,
        *new_out,
        *new_mlp,
        *new_down,
        *new_gains,
        *new_taps,
    )


def solution(mesh):
    fine = Mesh(mesh.devices.reshape(2, 4, 4, 2, 2), ALL)
    wt = ("yl", "core")
    acts = P(wt, SEQ, None)
    cube = P(wt, None, SEQ)
    flat_w = P(wt, SEQ)
    weights = (cube, flat_w, cube, flat_w, P(), P())
    in_specs = (acts, acts) + weights * 3
    out_specs = (acts, acts)
    for spec in weights:
        out_specs = out_specs + (spec, spec, spec)
    return jax.shard_map(local, mesh=fine, in_specs=in_specs, out_specs=out_specs, check_vma=False)
```

```python
import jax
import jax.numpy as jnp
from jax import lax
from jax.experimental import pallas as pl
from jax.experimental.pallas import tpu as pltpu
from jax.sharding import Mesh
from jax.sharding import PartitionSpec as P

D = 1024
FF = 4608
KERNEL = 3
STEP = 10

EPS = 1e-06
BETA_ONE = 0.9
BETA_TWO = 0.95
ADAM_EPS = 1e-08
DECAY = 0.1

SEQ = ("yh", "z", "x")
PLANE = ("z", "x")
ALL = ("yh", "z", "x", "yl", "core")
BF = jnp.bfloat16
F32 = jnp.float32


def flat(yh, z, x, w):
    return ((yh * 4 + z) * 4 + x) * 4 + w


def swapped_place(flip):
    pairs = []
    for s in range(32):
        for w in range(4):
            source = s * 4 + w
            pairs.append((source, flat((s & 1) ^ flip, w, (s >> 1) & 3, s >> 3)))
    return pairs


def straight_place(flip):
    pairs = []
    for s in range(32):
        for w in range(4):
            pairs.append((s * 4 + w, flat((s & 1) ^ flip, s >> 3, (s >> 1) & 3, w)))
    return pairs


def reverse(pairs):
    return [(b, a) for a, b in pairs]


def swap(v, axis):
    return lax.ppermute(v, axis, [(0, 1), (1, 0)])


def gather_group(own):
    far = swap(own, "yl")
    near = swap(own, "core")
    both = swap(far, "core")
    return jnp.stack([own, near, far, both])


def scatter_group(keep, low):
    near = swap(low, "core").astype(F32)
    half = keep[1] + near[1]
    far = swap(half.astype(BF), "yl").astype(F32)
    return keep[0] + near[0] + far


def tie(*values):
    return lax.optimization_barrier(values)


def in_order(near, far, yh):
    first = jnp.where(yh == 0, near, far)
    second = jnp.where(yh == 0, far, near)
    return jnp.stack([first, second])


def replace(first, second, pairs_of, yh):
    near = jnp.where(yh == 0, first, second)
    far = jnp.where(yh == 0, second, first)
    got_near = lax.ppermute(near, ALL, reverse(pairs_of(0)))
    got_far = lax.ppermute(far, ALL, reverse(pairs_of(1)))
    return got_near.astype(F32) + got_far.astype(F32)


def tn_kernel(a_ref, b_ref, out_ref):
    full = lax.dot_general(
        a_ref[...], b_ref[...], (((0,), (0,)), ((), ())), preferred_element_type=F32
    )
    for k in range(4):
        out_ref[k] = full[:, 256 * k : 256 * (k + 1)].astype(BF)


def dot_tn_blocked(a, b, step):
    rows, wide = a.shape
    return pl.pallas_call(
        tn_kernel,
        grid=(wide // step,),
        in_specs=[
            pl.BlockSpec((rows, step), lambda i: (0, i)),
            pl.BlockSpec((rows, D), lambda i: (0, 0)),
        ],
        out_specs=pl.BlockSpec((4, step, 256), lambda i: (0, i, 0)),
        out_shape=jax.ShapeDtypeStruct((4, wide, 256), BF),
        compiler_params=pltpu.CompilerParams(vmem_limit_bytes=40 * 1024 * 1024),
        cost_estimate=pl.CostEstimate(
            flops=2 * rows * wide * D,
            bytes_accessed=2 * (rows * wide + rows * D + wide * D),
            transcendentals=0,
        ),
    )(a, b)


def dot_nt(a, b):
    return lax.dot_general(a, b, (((1,), (1,)), ((), ())), preferred_element_type=F32)


def dot_nn(a, b):
    return lax.dot_general(a, b, (((1,), (0,)), ((), ())), preferred_element_type=F32)


def dot_tn(a, b):
    return lax.dot_general(a, b, (((0,), (0,)), ((), ())), preferred_element_type=F32)


def unit_rows(v):
    return v * lax.rsqrt(jnp.mean(v * v, axis=-1, keepdims=True) + EPS)


def in_part(w_ref, k, part):
    return w_ref[k, :, :, 32 * part : 32 * part + 32].reshape(256, 256)


def conv_kernel(
    tok_ref, halo_ref, gain_ref, tap_ref, w_ref, n_ref, p_ref, bx_ref, z_ref, y_ref, keep_ref, low_ref
):
    rows = n_ref.shape[1]
    tok = jnp.concatenate([halo_ref[0], tok_ref[0]], axis=0).astype(F32)
    normed = (unit_rows(tok) * gain_ref[0:1, :]).astype(BF)
    n_ref[0] = normed[16:]
    parts = []
    for part in range(3):
        weight = jnp.concatenate([in_part(w_ref, k, part) for k in range(4)], axis=1)
        parts.append(dot_nt(normed, weight))
        p_ref[0, part] = parts[part][16:]
    product = parts[0] * parts[2]
    bx_ref[0] = product
    conv = tap_ref[0:1, :] * product[16:]
    for k in range(1, KERNEL):
        conv = conv + tap_ref[k : k + 1, :] * product[16 - k : 16 - k + rows]
    z_ref[0] = conv
    mixed = (parts[1][16:] * conv).astype(BF)
    y_ref[0] = mixed
    put_part(dot_nt(mixed, w_ref[:, :, :, 96:128].reshape(D, 256)), keep_ref, low_ref)


def spec_of(shape, mode):
    tail = (0,) * (len(shape) - 1)
    if mode == "whole":
        return pl.BlockSpec(shape, lambda i: (0,) + tail)
    if mode == "two":
        return pl.BlockSpec((2,) + tuple(shape[1:]), lambda i: (i,) + tail)
    if mode == "pair":
        return pl.BlockSpec((1,) + tuple(shape[1:]), lambda i: (i // 2,) + tail)
    return pl.BlockSpec((1,) + tuple(shape[1:]), lambda i: (i,) + tail)


def grid_call(kernel, steps, ins, outs, flops, scratch=()):
    moved = sum(v.size * v.dtype.itemsize for v, _ in ins + outs)
    return pl.pallas_call(
        kernel,
        grid=(steps,),
        in_specs=[spec_of(v.shape, mode) for v, mode in ins],
        out_specs=[spec_of(v.shape, mode) for v, mode in outs],
        out_shape=[v for v, _ in outs],
        scratch_shapes=list(scratch),
        compiler_params=pltpu.CompilerParams(vmem_limit_bytes=56 * 1024 * 1024),
        cost_estimate=pl.CostEstimate(flops=flops, bytes_accessed=moved, transcendentals=0),
    )(*[v for v, _ in ins])


def put_part(value, keep_ref, low_ref):
    step = pl.program_id(0)

    @pl.when(step % 2 == 0)
    def _():
        keep_ref[0] = value

    @pl.when(step % 2 == 1)
    def _():
        low_ref[0] = value.astype(BF)


def ff_grad_kernel(g_ref, n_ref, c_ref, q_ref, out_ref):
    step = pl.program_id(0)
    for part in range(2):

        @pl.when(step == part)
        def _():
            full = lax.dot_general(
                g_ref[...], n_ref[...], (((0,), (0,)), ((), ())), preferred_element_type=F32
            ).astype(BF)
            for k in range(8):
                start = 288 * (k % 2) + 144 * part
                out_ref[k // 2, :, start : start + 144] = full[
                    :, 128 * k : 128 * (k + 1)
                ].reshape(8, 144, 128)

    @pl.when(step == 2)
    def _():
        full = lax.dot_general(
            c_ref[...], q_ref[...], (((0,), (0,)), ((), ())), preferred_element_type=F32
        ).astype(BF)
        for k in range(9):
            out_ref[:, :, 576 + 32 * k : 608 + 32 * k] = full[
                :, 128 * k : 128 * (k + 1)
            ].reshape(4, 8, 32, 128)


def ff_grads(g, n, c, q):
    rows, fw = q.shape
    return pl.pallas_call(
        ff_grad_kernel,
        grid=(3,),
        in_specs=[
            pl.BlockSpec((rows, fw), lambda i: (0, jnp.minimum(i, 1))),
            spec_of(n.shape, "whole"),
            spec_of(c.shape, "whole"),
            spec_of(q.shape, "whole"),
        ],
        out_specs=spec_of((4, 8, 864, 128), "whole"),
        out_shape=jax.ShapeDtypeStruct((4, 8, 864, 128), BF),
        compiler_params=pltpu.CompilerParams(vmem_limit_bytes=56 * 1024 * 1024),
        cost_estimate=pl.CostEstimate(
            flops=6 * rows * fw * D, bytes_accessed=19 * 1024 * 1024, transcendentals=0
        ),
    )(g, n, c, q)


def mlp_kernel(
    n_ref, c_ref, w_ref, q_ref, g_ref, down_ref, down_low, back_ref, back_low, up_w, down_w
):
    fw = FF // 4
    rows = n_ref.shape[1]

    @pl.when(pl.program_id(0) == 0)
    def _():
        for k in range(8):
            for part in range(2):
                start = 288 * (k % 2) + 144 * part
                up_w[fw * part : fw * (part + 1), 128 * k : 128 * (k + 1)] = w_ref[
                    k // 2, :, :, start : start + 144
                ].reshape(fw, 128)
        for k in range(9):
            down_w[:, 128 * k : 128 * (k + 1)] = w_ref[
                :, :, :, 576 + 32 * k : 608 + 32 * k
            ].reshape(D, 128)

    normed = n_ref[...].reshape(2 * rows, D)
    cot = c_ref[...].reshape(2 * rows, D)
    down = None
    back = None
    wide = 384
    for j in range(fw // wide):
        cols = slice(wide * j, wide * (j + 1))
        gate_w = up_w[wide * j : wide * (j + 1), :]
        lift_w = up_w[fw + wide * j : fw + wide * (j + 1), :]
        drop_w = down_w[:, cols]
        gate = dot_nt(normed, gate_w)
        lift = dot_nt(normed, lift_w)
        grad_hidden = dot_nn(cot, drop_w)
        sig = jax.nn.sigmoid(gate)
        swished = gate * sig
        hidden = (swished * lift).astype(BF)
        grad_lift = (grad_hidden * swished).astype(BF)
        grad_gate = (grad_hidden * lift * sig * (1.0 + gate * (1.0 - sig))).astype(BF)
        q_ref[:, :, cols] = hidden.reshape(2, rows, wide)
        g_ref[:, :, cols] = grad_gate.reshape(2, rows, wide)
        g_ref[:, :, fw + wide * j : fw + wide * (j + 1)] = grad_lift.reshape(2, rows, wide)
        more_down = dot_nt(hidden, drop_w)
        more_back = dot_nn(grad_gate, gate_w) + dot_nn(grad_lift, lift_w)
        down = more_down if j == 0 else down + more_down
        back = more_back if j == 0 else back + more_back
    down_ref[0] = down[:rows]
    down_low[0] = down[rows:].astype(BF)
    back_ref[0] = back[:rows]
    back_low[0] = back[rows:].astype(BF)


def mix_back_kernel(do_ref, w_ref, p_ref, z_ref, dz_ref, dc_ref):
    grad = dot_nn(do_ref[0], w_ref[:, :, :, 96:128].reshape(D, 256))
    dc_ref[0] = (grad * z_ref[0]).astype(BF)
    dz_ref[0] = grad * p_ref[0, 1]


def conv_back_kernel(
    dz_ref, after_ref, bx_ref, p_ref, dc_ref, tap_ref, tok_ref, w_ref, dp_ref, keep_ref, low_ref, gain_ref, gtap_ref
):
    rows = dz_ref.shape[1]
    dz = dz_ref[0]
    extended = jnp.concatenate([dz, after_ref[0]], axis=0)
    product = bx_ref[0]
    grad = tap_ref[0:1, :] * dz
    sums = [jnp.sum(dz * product[16:], axis=0, keepdims=True)]
    for k in range(1, KERNEL):
        grad = grad + tap_ref[k : k + 1, :] * extended[k : k + rows]
        sums.append(jnp.sum(dz * product[16 - k : 16 - k + rows], axis=0, keepdims=True))
    parts = [(grad * p_ref[0, 2]).astype(BF), dc_ref[0], (grad * p_ref[0, 0]).astype(BF)]
    for part in range(3):
        dp_ref[0, :, 256 * part : 256 * (part + 1)] = parts[part]
    all_parts = jnp.concatenate(parts, axis=1)
    hat = unit_rows(tok_ref[0].astype(F32))
    gains = []
    pieces = []
    for k in range(4):
        weight = jnp.concatenate([in_part(w_ref, k, part) for part in range(3)], axis=0)
        back = dot_nn(all_parts, weight)
        pieces.append(back)
        gains.append(
            jnp.sum(back * hat[:, 256 * k : 256 * (k + 1)], axis=0, keepdims=True)
        )
    put_part(jnp.concatenate(pieces, axis=1), keep_ref, low_ref)
    gain = jnp.concatenate(gains, axis=1)
    tap = jnp.concatenate(sums, axis=0)

    @pl.when(pl.program_id(0) == 0)
    def _():
        gain_ref[...] = gain
        gtap_ref[...] = tap

    @pl.when(pl.program_id(0) > 0)
    def _():
        gain_ref[...] += gain
        gtap_ref[...] += tap


def passed_along(shard, by):
    pairs = [(i, i + by) for i in range(32) if 0 <= i + by < 32]
    return lax.ppermute(shard, SEQ, pairs)


def norm_back(grad_hat, hat, scale):
    return scale * (grad_hat - hat * jnp.mean(grad_hat * hat, axis=-1, keepdims=True))


def adamw(weight, moment_one, moment_two, grad, rate, decay):
    new_one = BETA_ONE * moment_one + (1.0 - BETA_ONE) * grad
    new_two = BETA_TWO * moment_two + (1.0 - BETA_TWO) * grad * grad
    fixed_one = new_one / (1.0 - BETA_ONE**STEP)
    fixed_two = new_two / (1.0 - BETA_TWO**STEP)
    new_weight = weight - rate * (fixed_one / (jnp.sqrt(fixed_two) + ADAM_EPS) + decay * weight)
    return (new_one, new_two, new_weight)


def local(
    tokens,
    cotangent,
    w_in,
    w_out,
    w_mlp,
    w_down,
    gains,
    taps,
    m_in,
    m_out,
    m_mlp,
    m_down,
    m_gains,
    m_taps,
    v_in,
    v_out,
    v_mlp,
    v_down,
    v_gains,
    v_taps,
):
    rows = tokens.shape[1]
    yh = lax.axis_index("yh")
    wt = lax.axis_index(("yl", "core"))
    cw = D // 4
    fw = FF // 4

    t_in = w_in.astype(BF).transpose(1, 2, 0).reshape(96, 256)
    t_mlp = w_mlp.astype(BF).transpose(1, 2, 0).reshape(288, 256)
    t_out = w_out.astype(BF).T
    t_down = w_down.astype(BF).T
    own_toks = tokens[0]
    t_swapped = jnp.concatenate([t_in, t_mlp], axis=0)
    moved = [
        swap(own_toks, "yl"),
        swap(own_toks, "core"),
        passed_along(own_toks[rows - 16 :], 1),
        lax.ppermute(t_swapped, ALL, swapped_place(0)),
        lax.ppermute(t_swapped, ALL, swapped_place(1)),
        lax.ppermute(t_out, ALL, straight_place(0)),
        lax.ppermute(t_out, ALL, straight_place(1)),
        lax.ppermute(t_down, ALL, straight_place(0)),
        lax.ppermute(t_down, ALL, straight_place(1)),
    ]
    moved = tie(*moved)
    two_swapped = in_order(moved[3], moved[4], yh)
    two_out = in_order(moved[5], moved[6], yh)
    two_down = in_order(moved[7], moved[8], yh)
    two_conv = jnp.concatenate([two_swapped[:, :96], two_out], axis=1)
    mlp_rows = two_swapped[:, 96:]
    two_ff = jnp.concatenate(
        [mlp_rows[:, :, :128], mlp_rows[:, :, 128:]]
        + [two_down[:, :, 128 * k : 128 * (k + 1)] for k in range(9)],
        axis=1,
    )
    toks = jnp.stack([own_toks, moved[1], moved[0], swap(moved[0], "core")])
    halo = gather_group(moved[2])
    cots = gather_group(cotangent[0])

    sent = jnp.broadcast_to(two_conv.reshape(1, 256, 256), (16, 256, 256)).reshape(4096, 256)
    all_conv = lax.all_to_all(sent, PLANE, split_axis=0, concat_axis=0, tiled=True)
    all_conv = all_conv.reshape(4, 4, 2, 128, 256)
    all_ff = lax.all_gather(two_ff, PLANE, axis=0, tiled=False).reshape(4, 4, 2, 864, 128)

    own_taps = lax.dynamic_slice(taps, (0, wt * cw), (KERNEL, cw))
    shape = jax.ShapeDtypeStruct
    normed_one, parts, product, convolved, mixed, branch, branch_low = grid_call(
        conv_kernel,
        4,
        [
            (toks, "row"),
            (halo, "row"),
            (gains, "whole"),
            (own_taps, "whole"),
            (all_conv, "whole"),
        ],
        [
            (shape((4, rows, D), BF), "row"),
            (shape((4, 3, rows, cw), F32), "row"),
            (shape((4, rows + 16, cw), F32), "row"),
            (shape((4, rows, cw), F32), "row"),
            (shape((4, rows, cw), BF), "row"),
            (shape((2, rows, D), F32), "pair"),
            (shape((2, rows, D), BF), "pair"),
        ],
        8 * rows * D * D,
    )
    branch_low, cots = tie(branch_low, cots)
    residual = tokens[0].astype(F32) + scatter_group(branch, branch_low)
    scale_two = lax.rsqrt(jnp.mean(residual * residual, axis=-1, keepdims=True) + EPS)
    hat_two = residual * scale_two
    normed_two = gather_group((hat_two * gains[1]).astype(BF))
    hidden, grad_gu, down, down_low, back, back_low = grid_call(
        mlp_kernel,
        2,
        [(normed_two, "two"), (cots, "two"), (all_ff, "whole")],
        [
            (shape((4, rows, fw), BF), "two"),
            (shape((4, rows, 2 * fw), BF), "two"),
            (shape((2, rows, D), F32), "row"),
            (shape((2, rows, D), BF), "row"),
            (shape((2, rows, D), F32), "row"),
            (shape((2, rows, D), BF), "row"),
        ],
        48 * rows * D * fw,
        [pltpu.VMEM((2 * fw, D), BF), pltpu.VMEM((D, fw), BF)],
    )
    near = swap(back_low, "core").astype(F32)
    back_half = (back[1] + near[1]).astype(BF)
    down_near = swap(down_low, "core").astype(F32)
    down_half = (down[1] + down_near[1]).astype(BF)
    back_half, grad_gu = tie(back_half, grad_gu)
    back_far = swap(back_half, "yl")
    ff = ff_grads(
        grad_gu.reshape(4 * rows, 2 * fw),
        normed_two.reshape(4 * rows, D),
        cots.reshape(4 * rows, D),
        hidden.reshape(4 * rows, fw),
    )
    sum_ff = lax.psum_scatter(
        ff.reshape(16 * 1728, 128), PLANE, scatter_dimension=0, tiled=True
    ).reshape(2, 864, 128)
    grad_normed_two = back[0] + near[0] + back_far.astype(F32)
    gain_two = jnp.sum(grad_normed_two * hat_two, axis=0)
    grad_resid = cotangent[0].astype(F32) + norm_back(
        grad_normed_two * gains[1], hat_two, scale_two
    )
    branch_own, down_half = tie(grad_resid.astype(BF), down_half)
    branch_all = gather_group(branch_own)
    grad_conv, grad_c = grid_call(
        mix_back_kernel,
        4,
        [(branch_all, "row"), (all_conv, "whole"), (parts, "row"), (convolved, "row")],
        [(shape((4, rows, cw), F32), "row"), (shape((4, rows, cw), BF), "row")],
        2 * rows * D * D,
    )
    after = passed_along(grad_conv[:, :8], -1)
    grad_proj, part_one, part_low, gain_one, tap_sums = grid_call(
        conv_back_kernel,
        4,
        [
            (grad_conv, "row"),
            (after, "row"),
            (product, "row"),
            (parts, "row"),
            (grad_c, "row"),
            (own_taps, "whole"),
            (toks, "row"),
            (all_conv, "whole"),
        ],
        [
            (shape((4, rows, 3 * cw), BF), "row"),
            (shape((2, rows, D), F32), "pair"),
            (shape((2, rows, D), BF), "pair"),
            (shape((1, D), F32), "whole"),
            (shape((KERNEL, cw), F32), "whole"),
        ],
        6 * rows * D * D,
    )
    part_near = swap(part_low, "core").astype(F32)
    part_half = (part_one[1] + part_near[1]).astype(BF)
    grad_out = dot_tn(branch_all.reshape(4 * rows, D), mixed.reshape(4 * rows, cw)).astype(BF)
    grad_in = dot_tn_blocked(
        grad_proj.reshape(4 * rows, 3 * cw), normed_one.reshape(4 * rows, D), 384
    ).reshape(4, 3, 4, 2, 32, 256)
    grad_in = grad_in.transpose(0, 2, 3, 1, 4, 5).reshape(16, 192, 256)
    tap_full = lax.dynamic_update_slice(jnp.zeros((KERNEL, D), F32), tap_sums, (0, wt * cw))
    small = jnp.concatenate([gain_one, gain_two[None], tap_full], axis=0).reshape(20, 256)
    small = jnp.pad(small.astype(BF), ((0, 12), (0, 0)))
    grad_conv_w = jnp.concatenate(
        [grad_in, grad_out.reshape(16, 64, 256), jnp.broadcast_to(small[None], (16, 32, 256))],
        axis=1,
    )
    grad_conv_w, part_half, down_half = tie(grad_conv_w, part_half, down_half)
    part_far = swap(part_half, "yl")
    down_far = swap(down_half, "yl")
    got_conv = lax.all_to_all(
        grad_conv_w.reshape(16 * 288, 256), PLANE, split_axis=0, concat_axis=0, tiled=True
    )
    total_mlp = replace(sum_ff[0, :576], sum_ff[1, :576], swapped_place, yh)
    total_down = replace(sum_ff[0, 576:], sum_ff[1, 576:], straight_place, yh)
    block_out = residual + down[0] + down_near[0] + down_far.astype(F32)
    block_out = block_out.astype(BF)[None]
    grad_normed_one = part_one[0] + part_near[0] + part_far.astype(F32)
    tok_float = tokens[0].astype(F32)
    scale_one = lax.rsqrt(jnp.mean(tok_float * tok_float, axis=-1, keepdims=True) + EPS)
    hat_one = tok_float * scale_one
    grad_input = grad_resid + norm_back(grad_normed_one * gains[0], hat_one, scale_one)
    got_conv, total_mlp, total_down = tie(got_conv, total_mlp, total_down)
    sum_conv = jnp.sum(got_conv.reshape(16, 288, 256).astype(F32), axis=0)
    sum_low = sum_conv.astype(BF)
    total_in = replace(sum_low[:96], sum_low[96:192], swapped_place, yh)
    total_out = replace(sum_low[192:224], sum_low[224:256], straight_place, yh).T
    small = sum_conv[256:276]
    small = small + swap(small, "yh")
    others = [swap(small, "core"), swap(small, "yl")]
    others.append(lax.ppermute(small, ("yl", "core"), [(0, 3), (1, 2), (2, 1), (3, 0)]))
    small = (small + others[0] + others[1] + others[2]).reshape(5, D)
    total_mlp = total_mlp.reshape(2, 2, 144, 128).transpose(0, 3, 1, 2).reshape(256, 2, 144)
    total_down = total_down.reshape(9, 32, 128).transpose(0, 2, 1).reshape(fw, 32)
    total_in = total_in.reshape(3, 32, 256).transpose(2, 0, 1)
    new_in = adamw(w_in, m_in, v_in, total_in, 0.03, DECAY)
    new_out = adamw(w_out, m_out, v_out, total_out, 0.03, DECAY)
    new_mlp = adamw(w_mlp, m_mlp, v_mlp, total_mlp, 0.03, DECAY)
    new_down = adamw(w_down, m_down, v_down, total_down, 0.015, DECAY)
    new_gains = adamw(gains, m_gains, v_gains, small[:2], 0.6, 0.0)
    new_taps = adamw(taps, m_taps, v_taps, small[2:], 0.5, 0.0)
    return (
        block_out,
        grad_input[None],
        *new_in,
        *new_out,
        *new_mlp,
        *new_down,
        *new_gains,
        *new_taps,
    )


def solution(mesh):
    fine = Mesh(mesh.devices.reshape(2, 4, 4, 2, 2), ALL)
    wt = ("yl", "core")
    acts = P(wt, SEQ, None)
    cube = P(wt, None, SEQ)
    flat_w = P(wt, SEQ)
    weights = (cube, flat_w, cube, flat_w, P(), P())
    in_specs = (acts, acts) + weights * 3
    out_specs = (acts, acts)
    for spec in weights:
        out_specs = out_specs + (spec, spec, spec)
    return jax.shard_map(local, mesh=fine, in_specs=in_specs, out_specs=out_specs, check_vma=False)
```

```python
import jax
import jax.numpy as jnp
from jax import lax
from jax.experimental import pallas as pl
from jax.experimental.pallas import tpu as pltpu
from jax.sharding import Mesh
from jax.sharding import PartitionSpec as P

D = 1024
FF = 4608
KERNEL = 3
STEP = 10

EPS = 1e-06
BETA_ONE = 0.9
BETA_TWO = 0.95
ADAM_EPS = 1e-08
DECAY = 0.1

SEQ = ("yh", "z", "x")
PLANE = ("z", "x")
ALL = ("yh", "z", "x", "yl", "core")
BF = jnp.bfloat16
F32 = jnp.float32


def flat(yh, z, x, w):
    return ((yh * 4 + z) * 4 + x) * 4 + w


def swapped_place(flip):
    pairs = []
    for s in range(32):
        for w in range(4):
            source = s * 4 + w
            pairs.append((source, flat((s & 1) ^ flip, w, (s >> 1) & 3, s >> 3)))
    return pairs


def straight_place(flip):
    pairs = []
    for s in range(32):
        for w in range(4):
            pairs.append((s * 4 + w, flat((s & 1) ^ flip, s >> 3, (s >> 1) & 3, w)))
    return pairs


def reverse(pairs):
    return [(b, a) for a, b in pairs]


def swap(v, axis):
    return lax.ppermute(v, axis, [(0, 1), (1, 0)])


def gather_group(own):
    far = swap(own, "yl")
    near = swap(own, "core")
    both = swap(far, "core")
    return jnp.stack([own, near, far, both])


def scatter_group(keep, low):
    near = swap(low, "core").astype(F32)
    half = keep[1] + near[1]
    far = swap(half.astype(BF), "yl").astype(F32)
    return keep[0] + near[0] + far


def tie(*values):
    return lax.optimization_barrier(values)


def in_order(near, far, yh):
    first = jnp.where(yh == 0, near, far)
    second = jnp.where(yh == 0, far, near)
    return jnp.stack([first, second])


def replace(first, second, pairs_of, yh):
    near = jnp.where(yh == 0, first, second)
    far = jnp.where(yh == 0, second, first)
    got_near = lax.ppermute(near, ALL, reverse(pairs_of(0)))
    got_far = lax.ppermute(far, ALL, reverse(pairs_of(1)))
    return got_near.astype(F32) + got_far.astype(F32)


def tn_kernel(a_ref, b_ref, out_ref):
    full = lax.dot_general(
        a_ref[...], b_ref[...], (((0,), (0,)), ((), ())), preferred_element_type=F32
    )
    for k in range(4):
        out_ref[k] = full[:, 256 * k : 256 * (k + 1)].astype(BF)


def dot_tn_blocked(a, b, step):
    rows, wide = a.shape
    return pl.pallas_call(
        tn_kernel,
        grid=(wide // step,),
        in_specs=[
            pl.BlockSpec((rows, step), lambda i: (0, i)),
            pl.BlockSpec((rows, D), lambda i: (0, 0)),
        ],
        out_specs=pl.BlockSpec((4, step, 256), lambda i: (0, i, 0)),
        out_shape=jax.ShapeDtypeStruct((4, wide, 256), BF),
        compiler_params=pltpu.CompilerParams(vmem_limit_bytes=40 * 1024 * 1024),
        cost_estimate=pl.CostEstimate(
            flops=2 * rows * wide * D,
            bytes_accessed=2 * (rows * wide + rows * D + wide * D),
            transcendentals=0,
        ),
    )(a, b)


def dot_nt(a, b):
    return lax.dot_general(a, b, (((1,), (1,)), ((), ())), preferred_element_type=F32)


def dot_nn(a, b):
    return lax.dot_general(a, b, (((1,), (0,)), ((), ())), preferred_element_type=F32)


def dot_tn(a, b):
    return lax.dot_general(a, b, (((0,), (0,)), ((), ())), preferred_element_type=F32)


def unit_rows(v):
    return v * lax.rsqrt(jnp.mean(v * v, axis=-1, keepdims=True) + EPS)


def in_part(w_ref, k, part):
    return w_ref[k, :, :, 32 * part : 32 * part + 32].reshape(256, 256)


def conv_kernel(
    tok_ref, halo_ref, gain_ref, tap_ref, w_ref, n_ref, p_ref, bx_ref, z_ref, y_ref, keep_ref, low_ref
):
    rows = n_ref.shape[1]
    tok = jnp.concatenate([halo_ref[0], tok_ref[0]], axis=0).astype(F32)
    normed = (unit_rows(tok) * gain_ref[0:1, :]).astype(BF)
    n_ref[0] = normed[16:]
    parts = []
    for part in range(3):
        weight = jnp.concatenate([in_part(w_ref, k, part) for k in range(4)], axis=1)
        parts.append(dot_nt(normed, weight))
        p_ref[0, part] = parts[part][16:]
    product = parts[0] * parts[2]
    bx_ref[0] = product
    conv = tap_ref[0:1, :] * product[16:]
    for k in range(1, KERNEL):
        conv = conv + tap_ref[k : k + 1, :] * product[16 - k : 16 - k + rows]
    z_ref[0] = conv
    mixed = (parts[1][16:] * conv).astype(BF)
    y_ref[0] = mixed
    put_part(dot_nt(mixed, w_ref[:, :, :, 96:128].reshape(D, 256)), keep_ref, low_ref)


def spec_of(shape, mode):
    tail = (0,) * (len(shape) - 1)
    if mode == "whole":
        return pl.BlockSpec(shape, lambda i: (0,) + tail)
    if mode == "two":
        return pl.BlockSpec((2,) + tuple(shape[1:]), lambda i: (i,) + tail)
    if mode == "pair":
        return pl.BlockSpec((1,) + tuple(shape[1:]), lambda i: (i // 2,) + tail)
    return pl.BlockSpec((1,) + tuple(shape[1:]), lambda i: (i,) + tail)


def grid_call(kernel, steps, ins, outs, flops, scratch=()):
    moved = sum(v.size * v.dtype.itemsize for v, _ in ins + outs)
    return pl.pallas_call(
        kernel,
        grid=(steps,),
        in_specs=[spec_of(v.shape, mode) for v, mode in ins],
        out_specs=[spec_of(v.shape, mode) for v, mode in outs],
        out_shape=[v for v, _ in outs],
        scratch_shapes=list(scratch),
        compiler_params=pltpu.CompilerParams(vmem_limit_bytes=56 * 1024 * 1024),
        cost_estimate=pl.CostEstimate(flops=flops, bytes_accessed=moved, transcendentals=0),
    )(*[v for v, _ in ins])


def put_part(value, keep_ref, low_ref):
    step = pl.program_id(0)

    @pl.when(step % 2 == 0)
    def _():
        keep_ref[0] = value

    @pl.when(step % 2 == 1)
    def _():
        low_ref[0] = value.astype(BF)


def ff_grad_kernel(g_ref, n_ref, c_ref, q_ref, out_ref):
    step = pl.program_id(0)
    for part in range(2):

        @pl.when(step == part)
        def _():
            full = lax.dot_general(
                g_ref[...], n_ref[...], (((0,), (0,)), ((), ())), preferred_element_type=F32
            ).astype(BF)
            for k in range(8):
                start = 288 * (k % 2) + 144 * part
                out_ref[k // 2, :, start : start + 144] = full[
                    :, 128 * k : 128 * (k + 1)
                ].reshape(8, 144, 128)

    @pl.when(step == 2)
    def _():
        full = lax.dot_general(
            c_ref[...], q_ref[...], (((0,), (0,)), ((), ())), preferred_element_type=F32
        ).astype(BF)
        for k in range(9):
            out_ref[:, :, 576 + 32 * k : 608 + 32 * k] = full[
                :, 128 * k : 128 * (k + 1)
            ].reshape(4, 8, 32, 128)


def ff_grads(g, n, c, q):
    rows, fw = q.shape
    return pl.pallas_call(
        ff_grad_kernel,
        grid=(3,),
        in_specs=[
            pl.BlockSpec((rows, fw), lambda i: (0, jnp.minimum(i, 1))),
            spec_of(n.shape, "whole"),
            spec_of(c.shape, "whole"),
            spec_of(q.shape, "whole"),
        ],
        out_specs=spec_of((4, 8, 864, 128), "whole"),
        out_shape=jax.ShapeDtypeStruct((4, 8, 864, 128), BF),
        compiler_params=pltpu.CompilerParams(vmem_limit_bytes=56 * 1024 * 1024),
        cost_estimate=pl.CostEstimate(
            flops=6 * rows * fw * D, bytes_accessed=19 * 1024 * 1024, transcendentals=0
        ),
    )(g, n, c, q)


def mlp_kernel(
    n_ref, c_ref, w_ref, q_ref, g_ref, down_ref, down_low, back_ref, back_low, up_w, down_w
):
    fw = FF // 4
    rows = n_ref.shape[1]

    @pl.when(pl.program_id(0) == 0)
    def _():
        for k in range(8):
            for part in range(2):
                start = 288 * (k % 2) + 144 * part
                up_w[fw * part : fw * (part + 1), 128 * k : 128 * (k + 1)] = w_ref[
                    k // 2, :, :, start : start + 144
                ].reshape(fw, 128)
        for k in range(9):
            down_w[:, 128 * k : 128 * (k + 1)] = w_ref[
                :, :, :, 576 + 32 * k : 608 + 32 * k
            ].reshape(D, 128)

    normed = n_ref[...].reshape(2 * rows, D)
    cot = c_ref[...].reshape(2 * rows, D)
    down = None
    back = None
    wide = 384
    for j in range(fw // wide):
        cols = slice(wide * j, wide * (j + 1))
        gate_w = up_w[wide * j : wide * (j + 1), :]
        lift_w = up_w[fw + wide * j : fw + wide * (j + 1), :]
        drop_w = down_w[:, cols]
        gate = dot_nt(normed, gate_w)
        lift = dot_nt(normed, lift_w)
        grad_hidden = dot_nn(cot, drop_w)
        sig = jax.nn.sigmoid(gate)
        swished = gate * sig
        hidden = (swished * lift).astype(BF)
        grad_lift = (grad_hidden * swished).astype(BF)
        grad_gate = (grad_hidden * lift * sig * (1.0 + gate * (1.0 - sig))).astype(BF)
        q_ref[:, :, cols] = hidden.reshape(2, rows, wide)
        g_ref[:, :, cols] = grad_gate.reshape(2, rows, wide)
        g_ref[:, :, fw + wide * j : fw + wide * (j + 1)] = grad_lift.reshape(2, rows, wide)
        more_down = dot_nt(hidden, drop_w)
        more_back = dot_nn(grad_gate, gate_w) + dot_nn(grad_lift, lift_w)
        down = more_down if j == 0 else down + more_down
        back = more_back if j == 0 else back + more_back
    down_ref[0] = down[:rows]
    down_low[0] = down[rows:].astype(BF)
    back_ref[0] = back[:rows]
    back_low[0] = back[rows:].astype(BF)


def mix_back_kernel(do_ref, w_ref, p_ref, z_ref, dz_ref, dc_ref):
    grad = dot_nn(do_ref[0], w_ref[:, :, :, 96:128].reshape(D, 256))
    dc_ref[0] = (grad * z_ref[0]).astype(BF)
    dz_ref[0] = grad * p_ref[0, 1]


def conv_back_kernel(
    dz_ref, after_ref, bx_ref, p_ref, dc_ref, tap_ref, tok_ref, w_ref, dp_ref, keep_ref, low_ref, gain_ref, gtap_ref
):
    rows = dz_ref.shape[1]
    dz = dz_ref[0]
    extended = jnp.concatenate([dz, after_ref[0]], axis=0)
    product = bx_ref[0]
    grad = tap_ref[0:1, :] * dz
    sums = [jnp.sum(dz * product[16:], axis=0, keepdims=True)]
    for k in range(1, KERNEL):
        grad = grad + tap_ref[k : k + 1, :] * extended[k : k + rows]
        sums.append(jnp.sum(dz * product[16 - k : 16 - k + rows], axis=0, keepdims=True))
    parts = [(grad * p_ref[0, 2]).astype(BF), dc_ref[0], (grad * p_ref[0, 0]).astype(BF)]
    for part in range(3):
        dp_ref[0, :, 256 * part : 256 * (part + 1)] = parts[part]
    all_parts = jnp.concatenate(parts, axis=1)
    hat = unit_rows(tok_ref[0].astype(F32))
    gains = []
    pieces = []
    for k in range(4):
        weight = jnp.concatenate([in_part(w_ref, k, part) for part in range(3)], axis=0)
        back = dot_nn(all_parts, weight)
        pieces.append(back)
        gains.append(
            jnp.sum(back * hat[:, 256 * k : 256 * (k + 1)], axis=0, keepdims=True)
        )
    put_part(jnp.concatenate(pieces, axis=1), keep_ref, low_ref)
    gain = jnp.concatenate(gains, axis=1)
    tap = jnp.concatenate(sums, axis=0)

    @pl.when(pl.program_id(0) == 0)
    def _():
        gain_ref[...] = gain
        gtap_ref[...] = tap

    @pl.when(pl.program_id(0) > 0)
    def _():
        gain_ref[...] += gain
        gtap_ref[...] += tap


def passed_along(shard, by):
    pairs = [(i, i + by) for i in range(32) if 0 <= i + by < 32]
    return lax.ppermute(shard, SEQ, pairs)


def norm_back(grad_hat, hat, scale):
    return scale * (grad_hat - hat * jnp.mean(grad_hat * hat, axis=-1, keepdims=True))


def adamw(weight, moment_one, moment_two, grad, rate, decay):
    new_one = BETA_ONE * moment_one + (1.0 - BETA_ONE) * grad
    new_two = BETA_TWO * moment_two + (1.0 - BETA_TWO) * grad * grad
    fixed_one = new_one / (1.0 - BETA_ONE**STEP)
    fixed_two = new_two / (1.0 - BETA_TWO**STEP)
    new_weight = weight - rate * (fixed_one / (jnp.sqrt(fixed_two) + ADAM_EPS) + decay * weight)
    return (new_one, new_two, new_weight)


def local(
    tokens,
    cotangent,
    w_in,
    w_out,
    w_mlp,
    w_down,
    gains,
    taps,
    m_in,
    m_out,
    m_mlp,
    m_down,
    m_gains,
    m_taps,
    v_in,
    v_out,
    v_mlp,
    v_down,
    v_gains,
    v_taps,
):
    rows = tokens.shape[1]
    yh = lax.axis_index("yh")
    wt = lax.axis_index(("yl", "core"))
    cw = D // 4
    fw = FF // 4

    t_in = w_in.astype(BF).transpose(1, 2, 0).reshape(96, 256)
    t_mlp = w_mlp.astype(BF).transpose(1, 2, 0).reshape(288, 256)
    t_out = w_out.astype(BF).T
    t_down = w_down.astype(BF).T
    own_toks = tokens[0]
    t_swapped = jnp.concatenate([t_in, t_mlp], axis=0)
    t_straight = jnp.concatenate([t_out, t_down], axis=1)
    moved = tie(
        swap(own_toks, "yl"),
        lax.ppermute(t_swapped, ALL, swapped_place(0)),
        lax.ppermute(t_swapped, ALL, swapped_place(1)),
        lax.ppermute(t_straight, ALL, straight_place(0)),
        lax.ppermute(t_straight, ALL, straight_place(1)),
        own_toks,
    )
    own_toks = moved[5]
    two_swapped = in_order(moved[1], moved[2], yh)
    two_straight = in_order(moved[3], moved[4], yh)
    two_out = two_straight[:, :, :256]
    two_down = two_straight[:, :, 256:]
    two_conv = jnp.concatenate([two_swapped[:, :96], two_out], axis=1)
    mlp_rows = two_swapped[:, 96:]
    two_ff = jnp.concatenate(
        [mlp_rows[:, :, :128], mlp_rows[:, :, 128:]]
        + [two_down[:, :, 128 * k : 128 * (k + 1)] for k in range(9)],
        axis=1,
    )
    toks = jnp.stack(
        [own_toks, swap(own_toks, "core"), moved[0], swap(moved[0], "core")]
    )
    halo = gather_group(passed_along(own_toks[rows - 16 :], 1))
    cots = gather_group(cotangent[0])

    sent = jnp.broadcast_to(two_conv.reshape(1, 256, 256), (16, 256, 256)).reshape(4096, 256)
    all_conv = lax.all_to_all(sent, PLANE, split_axis=0, concat_axis=0, tiled=True)
    all_conv = all_conv.reshape(4, 4, 2, 128, 256)
    all_ff = lax.all_gather(two_ff, PLANE, axis=0, tiled=False).reshape(4, 4, 2, 864, 128)

    own_taps = lax.dynamic_slice(taps, (0, wt * cw), (KERNEL, cw))
    shape = jax.ShapeDtypeStruct
    normed_one, parts, product, convolved, mixed, branch, branch_low = grid_call(
        conv_kernel,
        4,
        [
            (toks, "row"),
            (halo, "row"),
            (gains, "whole"),
            (own_taps, "whole"),
            (all_conv, "whole"),
        ],
        [
            (shape((4, rows, D), BF), "row"),
            (shape((4, 3, rows, cw), F32), "row"),
            (shape((4, rows + 16, cw), F32), "row"),
            (shape((4, rows, cw), F32), "row"),
            (shape((4, rows, cw), BF), "row"),
            (shape((2, rows, D), F32), "pair"),
            (shape((2, rows, D), BF), "pair"),
        ],
        8 * rows * D * D,
    )
    branch_low, cots = tie(branch_low, cots)
    residual = tokens[0].astype(F32) + scatter_group(branch, branch_low)
    scale_two = lax.rsqrt(jnp.mean(residual * residual, axis=-1, keepdims=True) + EPS)
    hat_two = residual * scale_two
    normed_two = gather_group((hat_two * gains[1]).astype(BF))
    hidden, grad_gu, down, down_low, back, back_low = grid_call(
        mlp_kernel,
        2,
        [(normed_two, "two"), (cots, "two"), (all_ff, "whole")],
        [
            (shape((4, rows, fw), BF), "two"),
            (shape((4, rows, 2 * fw), BF), "two"),
            (shape((2, rows, D), F32), "row"),
            (shape((2, rows, D), BF), "row"),
            (shape((2, rows, D), F32), "row"),
            (shape((2, rows, D), BF), "row"),
        ],
        48 * rows * D * fw,
        [pltpu.VMEM((2 * fw, D), BF), pltpu.VMEM((D, fw), BF)],
    )
    near = swap(back_low, "core").astype(F32)
    back_half = (back[1] + near[1]).astype(BF)
    down_near = swap(down_low, "core").astype(F32)
    down_half = (down[1] + down_near[1]).astype(BF)
    back_half, grad_gu = tie(back_half, grad_gu)
    back_far = swap(back_half, "yl")
    ff = ff_grads(
        grad_gu.reshape(4 * rows, 2 * fw),
        normed_two.reshape(4 * rows, D),
        cots.reshape(4 * rows, D),
        hidden.reshape(4 * rows, fw),
    )
    grad_normed_two = back[0] + near[0] + back_far.astype(F32)
    gain_two = jnp.sum(grad_normed_two * hat_two, axis=0)
    grad_resid = cotangent[0].astype(F32) + norm_back(
        grad_normed_two * gains[1], hat_two, scale_two
    )
    branch_own, down_half, ff = tie(grad_resid.astype(BF), down_half, ff)
    sum_ff = lax.psum_scatter(
        ff.reshape(16 * 1728, 128), PLANE, scatter_dimension=0, tiled=True
    ).reshape(2, 864, 128)
    branch_all = gather_group(branch_own)
    grad_conv, grad_c = grid_call(
        mix_back_kernel,
        4,
        [(branch_all, "row"), (all_conv, "whole"), (parts, "row"), (convolved, "row")],
        [(shape((4, rows, cw), F32), "row"), (shape((4, rows, cw), BF), "row")],
        2 * rows * D * D,
    )
    after = passed_along(grad_conv[:, :8], -1)
    grad_proj, part_one, part_low, gain_one, tap_sums = grid_call(
        conv_back_kernel,
        4,
        [
            (grad_conv, "row"),
            (after, "row"),
            (product, "row"),
            (parts, "row"),
            (grad_c, "row"),
            (own_taps, "whole"),
            (toks, "row"),
            (all_conv, "whole"),
        ],
        [
            (shape((4, rows, 3 * cw), BF), "row"),
            (shape((2, rows, D), F32), "pair"),
            (shape((2, rows, D), BF), "pair"),
            (shape((1, D), F32), "whole"),
            (shape((KERNEL, cw), F32), "whole"),
        ],
        6 * rows * D * D,
    )
    part_near = swap(part_low, "core").astype(F32)
    part_half = (part_one[1] + part_near[1]).astype(BF)
    grad_out = dot_tn(branch_all.reshape(4 * rows, D), mixed.reshape(4 * rows, cw)).astype(BF)
    grad_in = dot_tn_blocked(
        grad_proj.reshape(4 * rows, 3 * cw), normed_one.reshape(4 * rows, D), 384
    ).reshape(4, 3, 4, 2, 32, 256)
    grad_in = grad_in.transpose(0, 2, 3, 1, 4, 5).reshape(16, 192, 256)
    tap_full = lax.dynamic_update_slice(jnp.zeros((KERNEL, D), F32), tap_sums, (0, wt * cw))
    small = jnp.concatenate([gain_one, gain_two[None], tap_full], axis=0).reshape(20, 256)
    small = small + swap(small, "core")
    small = jnp.pad(small.astype(BF), ((0, 12), (0, 0)))
    grad_conv_w = jnp.concatenate(
        [grad_in, grad_out.reshape(16, 64, 256), jnp.broadcast_to(small[None], (16, 32, 256))],
        axis=1,
    )
    grad_conv_w, part_half, down_half = tie(grad_conv_w, part_half, down_half)
    part_far = swap(part_half, "yl")
    down_far = swap(down_half, "yl")
    got_conv = lax.all_to_all(
        grad_conv_w.reshape(16 * 288, 256), PLANE, split_axis=0, concat_axis=0, tiled=True
    )
    block_out = residual + down[0] + down_near[0] + down_far.astype(F32)
    block_out = block_out.astype(BF)[None]
    grad_normed_one = part_one[0] + part_near[0] + part_far.astype(F32)
    tok_float = tokens[0].astype(F32)
    scale_one = lax.rsqrt(jnp.mean(tok_float * tok_float, axis=-1, keepdims=True) + EPS)
    hat_one = tok_float * scale_one
    grad_input = grad_resid + norm_back(grad_normed_one * gains[0], hat_one, scale_one)
    sum_conv = jnp.sum(got_conv.reshape(16, 288, 256).astype(F32), axis=0)
    sum_low = sum_conv.astype(BF)
    small = sum_conv[256:276]
    small = small + swap(small, "yh")
    small = (small + swap(small, "yl")).reshape(5, D)
    halves = (slice(0, 128), slice(128, 256))
    swapped = [
        jnp.concatenate([sum_ff[i, :576]] + [sum_low[96 * i : 96 * i + 96, h] for h in halves])
        for i in range(2)
    ]
    straight = [
        jnp.concatenate(
            [sum_ff[i, 576:]] + [sum_low[192 + 32 * i : 224 + 32 * i, h] for h in halves]
        )
        for i in range(2)
    ]
    swapped = replace(*swapped, swapped_place, yh)
    straight = replace(*straight, straight_place, yh)
    total_mlp = swapped[:576]
    total_in = jnp.concatenate([swapped[576:672], swapped[672:]], axis=1)
    total_down = straight[:288]
    total_out = jnp.concatenate([straight[288:320], straight[320:]], axis=1).T
    total_mlp = total_mlp.reshape(2, 2, 144, 128).transpose(0, 3, 1, 2).reshape(256, 2, 144)
    total_down = total_down.reshape(9, 32, 128).transpose(0, 2, 1).reshape(fw, 32)
    total_in = total_in.reshape(3, 32, 256).transpose(2, 0, 1)
    new_in = adamw(w_in, m_in, v_in, total_in, 0.03, DECAY)
    new_out = adamw(w_out, m_out, v_out, total_out, 0.03, DECAY)
    new_mlp = adamw(w_mlp, m_mlp, v_mlp, total_mlp, 0.03, DECAY)
    new_down = adamw(w_down, m_down, v_down, total_down, 0.015, DECAY)
    new_gains = adamw(gains, m_gains, v_gains, small[:2], 0.6, 0.0)
    new_taps = adamw(taps, m_taps, v_taps, small[2:], 0.5, 0.0)
    return (
        block_out,
        grad_input[None],
        *new_in,
        *new_out,
        *new_mlp,
        *new_down,
        *new_gains,
        *new_taps,
    )


def solution(mesh):
    fine = Mesh(mesh.devices.reshape(2, 4, 4, 2, 2), ALL)
    wt = ("yl", "core")
    acts = P(wt, SEQ, None)
    cube = P(wt, None, SEQ)
    flat_w = P(wt, SEQ)
    weights = (cube, flat_w, cube, flat_w, P(), P())
    in_specs = (acts, acts) + weights * 3
    out_specs = (acts, acts)
    for spec in weights:
        out_specs = out_specs + (spec, spec, spec)
    return jax.shard_map(local, mesh=fine, in_specs=in_specs, out_specs=out_specs, check_vma=False)
```
